32 devices in a mesh: wide: 8 (over z, y), narrow: 2 (over x), rep: 2 (over core).
Axes of the slice: x: 2, y: 2, z: 4, core: 2. Of those that a mesh axis runs over, the one named last changes fastest.
Arguments:
- layer_input: bfloat16 [2, 32, 128, 44, 1024], P('rep', None, 'wide', 'narrow'), may hold values from -6 to 6
- output_cotangent: bfloat16 [2, 32, 128, 44, 1024], P('rep', None, 'wide', 'narrow'), may hold values from -6 to 6
- spectral_weight: bfloat16 [2, 1536, 24, 2, 32, 32], P('narrow', 'wide'), may hold values from -6 to 6
Outputs:
- input_gradient: bfloat16 [2, 32, 128, 44, 1024], P('rep', None, 'wide', 'narrow')
- weight_gradient: float32 [2, 1536, 24, 2, 32, 32], P('narrow', 'wide', 'rep')
The draws below stay inside these ranges and needn't reach their ends.
All inputs are finite; a program needn't handle non-finite values.
Results may differ from the reference program's by a relative error of at most 0.012.
Values may be sent and summed in bfloat16 or wider, within the bound.
A program may use at most 256 MiB of HBM per device.

```python
import math
import jax
import jax.numpy as jnp
from jax import lax

C = 32
MX = 12
MY = 12
MZ = 16
MT = 4
NX = 128
NY = 44
NZ = 64
NT = 16
SAMPLES = 2
PAIR_BLOCKS = 2
KZT = 128
KZL = 64
COMB = 1536
N_REP = 2


def levels(rng, extent, split, least, top_value):
    level = 1.0
    for dim, parts in split:
        draws = jax.random.uniform(jax.random.fold_in(jax.random.fold_in(rng, 6), dim), (parts,), jnp.float32, least / len(split), top_value / len(split))
        level = level * jnp.repeat(jnp.exp(draws), extent[dim] // parts).reshape((-1,) + (1,) * (len(extent) - 1 - dim))
    return level


def centred(rng, extent, scale, limit, pieces=(), kind=jnp.bfloat16):
    level = levels(rng, extent, pieces, -0.22, 0.18) if pieces else 1.0
    drawn = jax.random.normal(rng, extent, jnp.float32) * scale * level
    return jnp.minimum(jnp.maximum(drawn, -limit), limit).astype(kind)


def setup_inputs(seed: int = 0) -> dict:
    keys = jax.random.split(jax.random.key(seed), 4)
    return {
        "layer_input": centred(keys[0], (SAMPLES, C, NX, NY, NZ * NT), 1.0, 6.0, ((0, 2), (2, 8), (3, 2))),
        "output_cotangent": centred(keys[1], (SAMPLES, C, NX, NY, NZ * NT), 1.0, 6.0, ((0, 2), (2, 8), (3, 2))),
        "spectral_weight": centred(keys[2], (PAIR_BLOCKS, COMB, 2 * MX, 2, C, C), 1.0, 6.0, ((0, 2), (1, 8))),
    }


def kept_waves(length, modes):
    indices = jnp.arange(2 * modes, dtype=jnp.int32)
    return jnp.where(indices < modes, indices, indices + length - 2 * modes)

def phase_pair(length, modes):
    positions = jnp.arange(length, dtype=jnp.int32)
    phase_turns = positions[:, None] * kept_waves(length, modes)[None, :] % length
    phases = 2.0 * math.pi / length * phase_turns.astype(jnp.float32)
    return (jnp.cos(phases), jnp.sin(phases))

def forward_table(length, modes):
    cosine, sine_part = phase_pair(length, modes)
    twiddle = jnp.stack([jnp.stack([cosine, -sine_part], axis=-1), jnp.stack([sine_part, cosine], axis=-1)], axis=1)
    return twiddle.astype(jnp.bfloat16)

def inverse_table(length, modes):
    cosine, sine_part = phase_pair(length, modes)
    cos_rows = cosine.T
    sin_rows = sine_part.T
    twiddle = jnp.stack([jnp.stack([cos_rows, sin_rows], axis=-1), jnp.stack([-sin_rows, cos_rows], axis=-1)], axis=1)
    return twiddle.astype(jnp.bfloat16)

def plane_tables():
    positions = jnp.arange(NZ * NT, dtype=jnp.int32)
    depth_index = positions // NT
    moment = positions % NT
    pair_index = jnp.arange(2 * MZ * MT, dtype=jnp.int32)
    wave_z = kept_waves(NZ, MZ)[pair_index // MT]
    wave_t = pair_index % MT
    phase_turns = (depth_index[:, None] * wave_z[None, :] % NZ * NT + moment[:, None] * wave_t[None, :] % NT * NZ) % (NZ * NT)
    phases = 2.0 * math.pi / (NZ * NT) * phase_turns.astype(jnp.float32)
    norm_scale = 1.0 / math.sqrt(NX * NY * NZ * NT)
    cosine = norm_scale * jnp.cos(phases)
    sine_part = norm_scale * jnp.sin(phases)
    forward = jnp.concatenate([cosine, -sine_part], axis=1).astype(jnp.bfloat16)
    inverse = jnp.concatenate([cosine.T, -sine_part.T], axis=0).astype(jnp.bfloat16)
    doubled = jnp.where(wave_t == 0, 1.0, 2.0).astype(jnp.float32)
    factor = jnp.concatenate([doubled, doubled])
    return (forward, inverse, factor)

def plane_spectrum(field, forward, factor):
    result = jnp.dot(field.reshape(-1, NZ * NT), forward, preferred_element_type=jnp.float32) * factor
    return result.astype(jnp.bfloat16).reshape(C, NX, NY, 2, KZT)

def spectrum_rest(plane):
    blocks = plane.reshape(C, NX, NY, 2, PAIR_BLOCKS, KZL).astype(jnp.float32)
    along_y = jnp.einsum('cxyrbm,yrjs->cxbsjm', blocks, forward_table(NY, MY).astype(jnp.float32), precision=lax.Precision.HIGHEST)
    along_y = along_y.astype(jnp.bfloat16).reshape(C, NX, PAIR_BLOCKS, 2, COMB).astype(jnp.float32)
    along_x = jnp.einsum('cxbrq,xrks->bqksc', along_y, forward_table(NX, MX).astype(jnp.float32), precision=lax.Precision.HIGHEST)
    return along_x.astype(jnp.bfloat16)

def dual_modes(weight_full, grad_spec):
    grad_full = grad_spec.astype(jnp.float32)
    grad_real = grad_full[..., 0, :]
    grad_imag = grad_full[..., 1, :]
    weight_real = weight_full[..., 0, :, :]
    weight_imag = weight_full[..., 1, :, :]

    def contract(left, right):
        return jnp.einsum('bqkio,bqko->bqki', left, right, precision=lax.Precision.HIGHEST)
    real_part = contract(weight_real, grad_real) + contract(weight_imag, grad_imag)
    imag_part = contract(weight_real, grad_imag) - contract(weight_imag, grad_real)
    return jnp.stack([real_part, imag_part], axis=-2).astype(jnp.bfloat16)

def outer_terms(input_spec, grad_spec):
    in_real = input_spec[..., 0, :].astype(jnp.float32)[..., :, None]
    in_imag = input_spec[..., 1, :].astype(jnp.float32)[..., :, None]
    grad_real = grad_spec[..., 0, :].astype(jnp.float32)[..., None, :]
    grad_imag = grad_spec[..., 1, :].astype(jnp.float32)[..., None, :]
    real_part = in_real * grad_real + in_imag * grad_imag
    imag_part = in_real * grad_imag - in_imag * grad_real
    return jnp.stack([real_part, imag_part], axis=-3)

def inverse_rest(dual):
    along_x = jnp.einsum('bqksc,ksxr->cxbrq', dual.astype(jnp.float32), inverse_table(NX, MX).astype(jnp.float32), precision=lax.Precision.HIGHEST)
    along_x = along_x.astype(jnp.bfloat16).reshape(C, NX, PAIR_BLOCKS, 2, 2 * MY, KZL).astype(jnp.float32)
    along_y = jnp.einsum('cxbsjm,jsyr->cxyrbm', along_x, inverse_table(NY, MY).astype(jnp.float32), precision=lax.Precision.HIGHEST)
    return along_y.astype(jnp.bfloat16).reshape(C, NX, NY, 2, KZT)

def reference(layer_input, output_cotangent, spectral_weight):
    forward, inverse, factor = plane_tables()
    unit_factor = jnp.ones_like(factor)
    weight_full = spectral_weight.astype(jnp.float32)
    total = jnp.zeros((PAIR_BLOCKS, COMB, 2 * MX, 2, C, C), jnp.float32)
    gradients = []
    for sample in range(N_REP):
        input_spec = spectrum_rest(plane_spectrum(layer_input[sample], forward, unit_factor))
        grad_spec = spectrum_rest(plane_spectrum(output_cotangent[sample], forward, factor))
        total = total + outer_terms(input_spec, grad_spec)
        back_plane = inverse_rest(dual_modes(weight_full, grad_spec))
        field = jnp.dot(back_plane.reshape(-1, 2 * KZT), inverse, preferred_element_type=jnp.float32)
        gradients.append(field.astype(jnp.bfloat16).reshape(C, NX, NY, NZ * NT))
    return (jnp.stack(gradients), total)
```

```python
import functools
import math

import jax
import jax.numpy as jnp
import ml_dtypes
import numpy as np
from jax import lax
from jax.experimental import pallas as pl
from jax.experimental.pallas import tpu as pltpu
from jax.sharding import PartitionSpec as P

MX = 12
MY = 12
MZ = 16
MT = 4
NX = 128
NY = 44
NZ = 64
NT = 16

CHANNEL_STEP = 4
SPEC_STEP = 16
GRAD_CHUNKS = 1
INPUT_CHUNKS = 1
BACK_CHUNKS = 1
VMEM_BYTES = 48 * 1024 * 1024


def kept_waves(length, modes):
    indices = jnp.arange(2 * modes, dtype=jnp.int32)
    return jnp.where(indices < modes, indices, indices + length - 2 * modes)


def phase_pair(length, modes):
    positions = jnp.arange(length, dtype=jnp.int32)
    phase_turns = positions[:, None] * kept_waves(length, modes)[None, :] % length
    phases = 2.0 * math.pi / length * phase_turns.astype(jnp.float32)
    return (jnp.cos(phases), jnp.sin(phases))


def forward_table(length, modes):
    cosine, sine_part = phase_pair(length, modes)
    twiddle = jnp.stack(
        [jnp.stack([cosine, -sine_part], axis=-1), jnp.stack([sine_part, cosine], axis=-1)], axis=1
    )
    return twiddle.astype(jnp.bfloat16)


def inverse_table(length, modes):
    cosine, sine_part = phase_pair(length, modes)
    cos_rows = cosine.T
    sin_rows = sine_part.T
    twiddle = jnp.stack(
        [jnp.stack([cos_rows, sin_rows], axis=-1), jnp.stack([-sin_rows, cos_rows], axis=-1)],
        axis=1,
    )
    return twiddle.astype(jnp.bfloat16)


def plane_tables():
    positions = jnp.arange(NZ * NT, dtype=jnp.int32)
    depth_index = positions // NT
    moment = positions % NT
    pair_index = jnp.arange(2 * MZ * MT, dtype=jnp.int32)
    wave_z = kept_waves(NZ, MZ)[pair_index // MT]
    wave_t = pair_index % MT
    phase_turns = (
        depth_index[:, None] * wave_z[None, :] % NZ * NT
        + moment[:, None] * wave_t[None, :] % NT * NZ
    ) % (NZ * NT)
    phases = 2.0 * math.pi / (NZ * NT) * phase_turns.astype(jnp.float32)
    norm_scale = 1.0 / math.sqrt(NX * NY * NZ * NT)
    cosine = norm_scale * jnp.cos(phases)
    sine_part = norm_scale * jnp.sin(phases)
    forward = jnp.concatenate([cosine, -sine_part], axis=1).astype(jnp.bfloat16)
    inverse = jnp.concatenate([cosine.T, -sine_part.T], axis=0).astype(jnp.bfloat16)
    doubled = jnp.where(wave_t == 0, 1.0, 2.0).astype(jnp.float32)
    factor = jnp.concatenate([doubled, doubled])
    return (forward, inverse, factor)


def outer_terms(input_spec, grad_spec):
    in_real = input_spec[..., 0, :].astype(jnp.float32)[..., :, None]
    in_imag = input_spec[..., 1, :].astype(jnp.float32)[..., :, None]
    grad_real = grad_spec[..., 0, :].astype(jnp.float32)[..., None, :]
    grad_imag = grad_spec[..., 1, :].astype(jnp.float32)[..., None, :]
    real_part = in_real * grad_real + in_imag * grad_imag
    imag_part = in_real * grad_imag - in_imag * grad_real
    return jnp.stack([real_part, imag_part], axis=-3)


def shards(layer_input, output_cotangent, spectral_weight):
    input_field = layer_input[0]
    grad_field = output_cotangent[0]
    channels, local_x, local_y, plane_cells = grad_field.shape
    pair_count = 2 * MZ * MT
    forward, inverse, factor = plane_tables()
    input_plane = jnp.dot(
        input_field.reshape(-1, plane_cells), forward, preferred_element_type=jnp.float32
    )
    input_plane = input_plane.astype(jnp.bfloat16).reshape(
        channels, local_x, local_y, 2, pair_count
    )
    grad_plane = (
        jnp.dot(grad_field.reshape(-1, plane_cells), forward, preferred_element_type=jnp.float32)
        * factor
    )
    grad_plane = grad_plane.astype(jnp.bfloat16).reshape(channels, local_x, local_y, 2, pair_count)
    table_y = forward_table(NY, MY)
    fields = (
        lax.all_to_all(input_plane, "narrow", split_axis=4, concat_axis=2, tiled=True),
        lax.all_to_all(grad_plane, "narrow", split_axis=4, concat_axis=2, tiled=True),
    )
    input_line, grad_line = tuple(
        (
            jnp.einsum(
                "cxyrm,yrjs->cxsjm", field, table_y, preferred_element_type=jnp.float32
            ).astype(jnp.bfloat16)
            for field in fields
        )
    )
    combos = input_line.shape[3] * input_line.shape[4]
    input_flat = input_line.reshape(channels, local_x, 2, combos)
    grad_flat = grad_line.reshape(channels, local_x, 2, combos)
    table_x = forward_table(NX, MX)
    back_table_x = inverse_table(NX, MX)
    back_table_y = inverse_table(NY, MY)
    fields = (
        lax.all_to_all(input_flat, "wide", split_axis=3, concat_axis=1, tiled=True),
        lax.all_to_all(grad_flat, "wide", split_axis=3, concat_axis=1, tiled=True),
    )
    input_spec, grad_spec = tuple(
        (
            jnp.einsum(
                "cxrq,xrks->qksc", field, table_x, preferred_element_type=jnp.float32
            ).astype(jnp.bfloat16)
            for field in fields
        )
    )
    weight_block = spectral_weight[0]
    weight_real = weight_block[:, :, 0]
    weight_imag = weight_block[:, :, 1]
    grad_real = grad_spec[:, :, 0]
    grad_imag = grad_spec[:, :, 1]

    def contract(left, right):
        return jnp.einsum("qkio,qko->qki", left, right, preferred_element_type=jnp.float32)

    dual_real = contract(weight_real, grad_real) + contract(weight_imag, grad_imag)
    dual_imag = contract(weight_real, grad_imag) - contract(weight_imag, grad_real)
    dual = jnp.stack([dual_real, dual_imag], axis=2).astype(jnp.bfloat16)
    both_input, both_grad = (
        lax.all_gather(input_spec[None], "rep", axis=0, tiled=True),
        lax.all_gather(grad_spec[None], "rep", axis=0, tiled=True),
    )
    half_modes = input_spec.shape[1] // lax.axis_size("rep")
    mode_start = lax.axis_index("rep") * half_modes
    input_half = lax.dynamic_slice_in_dim(both_input, mode_start, half_modes, 2)
    grad_half = lax.dynamic_slice_in_dim(both_grad, mode_start, half_modes, 2)
    weight_grad = jnp.sum(outer_terms(input_half, grad_half), axis=0)
    back_x = jnp.einsum(
        "qksc,ksxr->cxrq", dual, back_table_x, preferred_element_type=jnp.float32
    ).astype(jnp.bfloat16)
    block_part = lax.all_to_all(back_x, "wide", split_axis=1, concat_axis=3, tiled=True)
    shaped = block_part.reshape(block_part.shape[0], local_x, 2, 2 * MY, -1)
    back_line = jnp.einsum(
        "cxsjm,jsyr->cxyrm", shaped, back_table_y, preferred_element_type=jnp.float32
    ).astype(jnp.bfloat16)
    block_part = lax.all_to_all(back_line, "narrow", split_axis=2, concat_axis=4, tiled=True)
    result = jnp.dot(
        block_part.reshape(-1, 2 * pair_count), inverse, preferred_element_type=jnp.float32
    )
    input_grad = result.astype(jnp.bfloat16).reshape(
        block_part.shape[0], local_x, local_y, plane_cells
    )
    return (input_grad[None], weight_grad[None])


def np_phases(length, modes):
    waves = np.arange(2 * modes)
    waves = np.where(waves < modes, waves, waves + length - 2 * modes)
    turns = np.arange(length)[:, None] * waves[None, :] % length
    phases = np.float32(2.0 * math.pi / length) * turns.astype(np.float32)
    return (np.cos(phases), np.sin(phases))


def np_plane(blocks):
    positions = np.arange(NZ * NT)
    pairs = np.arange(2 * MZ * MT)
    waves = np.arange(2 * MZ)
    waves = np.where(waves < MZ, waves, waves + NZ - 2 * MZ)[pairs // MT]
    moments = pairs % MT
    turns = (
        (positions // NT)[:, None] * waves[None, :] % NZ * NT
        + (positions % NT)[:, None] * moments[None, :] % NT * NZ
    ) % (NZ * NT)
    phases = np.float32(2.0 * math.pi / (NZ * NT)) * turns.astype(np.float32)
    scale = np.float32(1.0 / math.sqrt(NX * NY * NZ * NT))
    cells = NZ * NT
    cosine = (scale * np.cos(phases)).reshape(cells, blocks, -1)
    sine = (scale * np.sin(phases)).reshape(cells, blocks, -1)
    factor = np.where(moments == 0, 1.0, 2.0).astype(np.float32).reshape(blocks, -1)
    return cosine, sine, factor


def pick(options, index):
    return lax.dynamic_index_in_dim(jnp.asarray(np.stack(options)), index, 0, keepdims=False)


def bf16(array):
    return np.asarray(array, np.float32).astype(ml_dtypes.bfloat16)


def zt_tables(order):
    cosine, sine, factor = np_plane(len(order))
    both = np.stack([cosine, -sine], axis=2)[:, order]
    plain = bf16(both)
    grad = bf16(plain.astype(np.float32) * factor[order][None, :, None, :])
    cells = both.shape[0]
    plain = plain.reshape(cells, -1)
    return plain, grad.reshape(cells, -1), np.ascontiguousarray(plain.T)


def y_tables(order, local_y, local_x):
    cosine, sine = np_phases(NY, MY)
    both = bf16(np.stack([cosine, sine])).astype(np.float32)
    rows = np.concatenate([np.arange(o * local_y, (o + 1) * local_y) for o in order])
    both = both[:, rows]
    eye = np.eye(local_x, dtype=np.float32)
    forward = np.einsum("ayj,xz->ajxyz", both, eye).reshape(2 * 2 * MY * local_x, -1)
    back = np.einsum("ayj,xz->ayxjz", both, eye).reshape(2 * NY * local_x, -1)
    return bf16(forward), bf16(back)


def x_tables():
    cosine, sine = np_phases(NX, MX)
    forward = np.concatenate([cosine.T, sine.T], axis=0)
    back = np.concatenate([cosine, sine], axis=0)
    return bf16(forward), bf16(back)


def params():
    return pltpu.CompilerParams(vmem_limit_bytes=VMEM_BYTES)


def cost(flops, moved):
    return pl.CostEstimate(flops=int(flops), bytes_accessed=int(moved), transcendentals=0)


def signs(shape, first):
    lane = lax.broadcasted_iota(jnp.int32, shape, 1)
    return jnp.where(lane < shape[1] // 2, first, -first).astype(jnp.float32)


def half_turn(array):
    return pltpu.roll(array, array.shape[1] // 2, 1)


def plane_kernel(field_ref, table_ref, own_ref, other_ref):
    lanes = own_ref.shape[1]
    result = jnp.dot(field_ref[...], table_ref[...], preferred_element_type=jnp.float32)
    result = result.astype(jnp.bfloat16)
    own_ref[...] = result[:, :lanes]
    other_ref[...] = result[:, lanes:]


def plane_call(field, table, start, count, rows):
    step = CHANNEL_STEP
    cells, columns = table.shape
    lanes = columns // 2
    shape = jax.ShapeDtypeStruct((count * rows, lanes), jnp.bfloat16)
    out_spec = pl.BlockSpec((step * rows, lanes), lambda i: (i, 0))
    return pl.pallas_call(
        plane_kernel,
        grid=(count // step,),
        in_specs=[
            pl.BlockSpec((step * rows, cells), lambda i: (start // step + i, 0)),
            pl.BlockSpec((cells, columns), lambda i: (0, 0)),
        ],
        out_specs=[out_spec, out_spec],
        out_shape=[shape, shape],
        compiler_params=params(),
        cost_estimate=cost(2 * count * rows * cells * columns, 2 * count * rows * (cells + columns)),
        name="plane",
    )(field, table)


def line_kernel(rows, own_ref, recv_ref, table_ref, out_ref):
    wide, channels, part, lanes = out_ref.shape
    half = wide * part
    sign = signs((half, lanes), 1.0)
    for pair in range(0, channels, 2):
        data = jnp.concatenate(
            [
                jnp.concatenate(
                    [own_ref[c * rows : (c + 1) * rows], recv_ref[c * rows : (c + 1) * rows]], axis=0
                )
                for c in (pair, pair + 1)
            ],
            axis=1,
        )
        result = jnp.dot(table_ref[...], data, preferred_element_type=jnp.float32)
        for at in range(2):
            block = result[:, at * lanes : (at + 1) * lanes]
            line = (block[:half] + sign * half_turn(block[half:])).astype(jnp.bfloat16)
            for w in range(wide):
                out_ref[w, pair + at] = line[w * part : (w + 1) * part]


def line_call(own, recv, table, wide, rows):
    step = CHANNEL_STEP
    count = own.shape[0] // rows
    lanes = own.shape[1]
    half = table.shape[0] // 2
    in_spec = pl.BlockSpec((step * rows, lanes), lambda i: (i, 0))
    return pl.pallas_call(
        functools.partial(line_kernel, rows),
        grid=(count // step,),
        in_specs=[in_spec, in_spec, pl.BlockSpec(table.shape, lambda i: (0, 0))],
        out_specs=pl.BlockSpec((wide, step, half // wide, lanes), lambda i: (0, i, 0, 0)),
        out_shape=jax.ShapeDtypeStruct((wide, count, half // wide, lanes), jnp.bfloat16),
        compiler_params=params(),
        cost_estimate=cost(4 * count * half * table.shape[1] * lanes, 2 * count * lanes * (half + table.shape[1])),
        name="line",
    )(own, recv, table)


def spec_kernel(local_x, data_ref, table_ref, out_ref, held):
    wide, channels, part, lanes = data_ref.shape
    combos = part // local_x
    kept = table_ref.shape[0] // 2
    pairs = lanes // 2
    sign = signs((kept, lanes), 1.0)
    low = lax.broadcasted_iota(jnp.int32, (kept, lanes), 1) < pairs
    for c in range(channels):
        data = jnp.concatenate(
            [
                jnp.concatenate(
                    [data_ref[w, c, j * local_x : (j + 1) * local_x] for w in range(wide)], axis=0
                )
                for j in range(combos)
            ],
            axis=1,
        )
        result = jnp.dot(table_ref[...], data, preferred_element_type=jnp.float32)
        parts = []
        for j in range(combos):
            block = result[:, j * lanes : (j + 1) * lanes]
            parts.append(block[:kept] + sign * half_turn(block[kept:]))
        for j in range(0, combos - 1, 2):
            first, second = parts[j], parts[j + 1]
            held[:, 0, c, j * pairs : (j + 2) * pairs] = jnp.where(low, first, half_turn(second))
            held[:, 1, c, j * pairs : (j + 2) * pairs] = jnp.where(low, half_turn(first), second)
        if combos % 2:
            j = combos - 1
            held[:, 0, c, j * pairs : (j + 1) * pairs] = parts[j][:, :pairs]
            held[:, 1, c, j * pairs : (j + 1) * pairs] = half_turn(parts[j])[:, :pairs]
    out_ref[...] = held[...].astype(jnp.bfloat16)


def spec_call(data, table, local_x):
    wide, count, part, lanes = data.shape
    step = SPEC_STEP
    kept = table.shape[0] // 2
    width = part // local_x * lanes // 2
    return pl.pallas_call(
        functools.partial(spec_kernel, local_x),
        grid=(count // step,),
        in_specs=[
            pl.BlockSpec((wide, step, part, lanes), lambda i: (0, i, 0, 0)),
            pl.BlockSpec(table.shape, lambda i: (0, 0)),
        ],
        out_specs=pl.BlockSpec((kept, 2, step, width), lambda i: (0, 0, i, 0)),
        out_shape=jax.ShapeDtypeStruct((kept, 2, count, width), jnp.bfloat16),
        scratch_shapes=[pltpu.VMEM((kept, 2, step, width), jnp.float32)],
        compiler_params=params(),
        cost_estimate=cost(4 * count * kept * table.shape[1] * 2 * width, 2 * data.size + 4 * kept * count * width),
        name="spec",
    )(data, table)


def dual_kernel(weight_ref, grad_ref, out_ref):
    inputs = weight_ref.shape[2]
    grad_real = grad_ref[0, 0].astype(jnp.float32)
    grad_imag = grad_ref[0, 1].astype(jnp.float32)
    for i in range(0, inputs, 8):
        real = weight_ref[0, 0, i : i + 8].astype(jnp.float32)
        imag = weight_ref[0, 1, i : i + 8].astype(jnp.float32)
        dual_real = jnp.sum(real * grad_real[None] + imag * grad_imag[None], axis=1)
        dual_imag = jnp.sum(real * grad_imag[None] - imag * grad_real[None], axis=1)
        out_ref[0, 0, i : i + 8] = dual_real.astype(jnp.bfloat16).astype(jnp.float32)
        out_ref[0, 1, i : i + 8] = dual_imag.astype(jnp.bfloat16).astype(jnp.float32)


def dual_call(weight, grad):
    kept, parts, inputs, outputs, width = weight.shape
    return pl.pallas_call(
        dual_kernel,
        grid=(kept,),
        in_specs=[
            pl.BlockSpec((1, parts, inputs, outputs, width), lambda k: (k, 0, 0, 0, 0)),
            pl.BlockSpec((1, parts, outputs, width), lambda k: (k, 0, 0, 0)),
        ],
        out_specs=pl.BlockSpec((1, parts, inputs, width), lambda k: (k, 0, 0, 0)),
        out_shape=jax.ShapeDtypeStruct((kept, parts, inputs, width), jnp.float32),
        compiler_params=params(),
        cost_estimate=cost(4 * weight.size, 2 * weight.size),
        name="dual",
    )(weight, grad)


def outer_kernel(input_ref, grad_ref, out_ref):
    samples = input_ref.shape[0]
    inputs = out_ref.shape[2]
    for i in range(0, inputs, 8):
        real_part = 0.0
        imag_part = 0.0
        for n in range(samples):
            in_real = input_ref[n, 0, 0, i : i + 8].astype(jnp.float32)[:, None, :]
            in_imag = input_ref[n, 0, 1, i : i + 8].astype(jnp.float32)[:, None, :]
            grad_real = grad_ref[n, 0, 0].astype(jnp.float32)[None]
            grad_imag = grad_ref[n, 0, 1].astype(jnp.float32)[None]
            real_part = real_part + (in_real * grad_real + in_imag * grad_imag)
            imag_part = imag_part + (in_real * grad_imag - in_imag * grad_real)
        out_ref[0, 0, i : i + 8] = real_part
        out_ref[0, 1, i : i + 8] = imag_part


def outer_call(both_input, both_grad):
    samples, kept, parts, channels, width = both_input.shape
    in_spec = pl.BlockSpec((samples, 1, parts, channels, width), lambda k: (0, k, 0, 0, 0))
    out = (kept, parts, channels, channels, width)
    return pl.pallas_call(
        outer_kernel,
        grid=(kept,),
        in_specs=[in_spec, in_spec],
        out_specs=pl.BlockSpec((1,) + out[1:], lambda k: (k, 0, 0, 0, 0)),
        out_shape=jax.ShapeDtypeStruct(out, jnp.float32),
        compiler_params=params(),
        cost_estimate=cost(8 * math.prod(out), 6 * math.prod(out)),
        name="outer",
    )(both_input, both_grad)


def back_x_kernel(local_x, dual_ref, table_ref, out_ref):
    wide, channels, part, lanes = out_ref.shape
    combos = part // local_x
    kept = dual_ref.shape[0]
    pairs = lanes // 2
    cells = wide * local_x
    sign = signs((cells, lanes), -1.0)
    low = lax.broadcasted_iota(jnp.int32, (kept, lanes), 1) < pairs
    for c in range(channels):
        blocks = []
        for j in range(0, combos - 1, 2):
            real = dual_ref[:, 0, c, j * pairs : (j + 2) * pairs]
            imag = dual_ref[:, 1, c, j * pairs : (j + 2) * pairs]
            blocks.append(jnp.where(low, real, half_turn(imag)))
            blocks.append(jnp.where(low, half_turn(real), imag))
        if combos % 2:
            j = combos - 1
            real = dual_ref[:, 0, c, j * pairs : (j + 1) * pairs]
            imag = dual_ref[:, 1, c, j * pairs : (j + 1) * pairs]
            blocks.append(jnp.concatenate([real, imag], axis=1))
        data = jnp.concatenate(blocks, axis=1).astype(jnp.bfloat16)
        result = jnp.dot(table_ref[...], data, preferred_element_type=jnp.float32)
        for j in range(combos):
            block = result[:, j * lanes : (j + 1) * lanes]
            back = (block[:cells] + sign * half_turn(block[cells:])).astype(jnp.bfloat16)
            for w in range(wide):
                out_ref[w, c, j * local_x : (j + 1) * local_x] = back[w * local_x : (w + 1) * local_x]


def back_x_call(dual, table, wide, local_x, pairs, start, count):
    kept, parts, channels, width = dual.shape
    step = 8
    part = width // pairs * local_x
    lanes = 2 * pairs
    return pl.pallas_call(
        functools.partial(back_x_kernel, local_x),
        grid=(count // step,),
        in_specs=[
            pl.BlockSpec((kept, parts, step, width), lambda i: (0, 0, start // step + i, 0)),
            pl.BlockSpec(table.shape, lambda i: (0, 0)),
        ],
        out_specs=pl.BlockSpec((wide, step, part, lanes), lambda i: (0, i, 0, 0)),
        out_shape=jax.ShapeDtypeStruct((wide, count, part, lanes), jnp.bfloat16),
        compiler_params=params(),
        cost_estimate=cost(4 * count * kept * table.shape[0] * width, 4 * kept * count * width * 2),
        name="back_x",
    )(dual, table)


def back_y_kernel(rows, data_ref, table_ref, own_ref, other_ref):
    wide, channels, part, lanes = data_ref.shape
    half = table_ref.shape[0] // 2
    sign = signs((half, lanes), -1.0)
    for pair in range(0, channels, 2):
        data = jnp.concatenate(
            [
                jnp.concatenate([data_ref[w, c] for w in range(wide)], axis=0)
                for c in (pair, pair + 1)
            ],
            axis=1,
        )
        result = jnp.dot(table_ref[...], data, preferred_element_type=jnp.float32)
        for at in range(2):
            c = pair + at
            block = result[:, at * lanes : (at + 1) * lanes]
            back = (block[:half] + sign * half_turn(block[half:])).astype(jnp.bfloat16)
            own_ref[c * rows : (c + 1) * rows] = back[:rows]
            other_ref[c * rows : (c + 1) * rows] = back[rows:]


def back_y_call(data, table, rows):
    wide, count, part, lanes = data.shape
    step = CHANNEL_STEP
    shape = jax.ShapeDtypeStruct((count * rows, lanes), jnp.bfloat16)
    out_spec = pl.BlockSpec((step * rows, lanes), lambda i: (i, 0))
    return pl.pallas_call(
        functools.partial(back_y_kernel, rows),
        grid=(count // step,),
        in_specs=[
            pl.BlockSpec((wide, step, part, lanes), lambda i: (0, i, 0, 0)),
            pl.BlockSpec(table.shape, lambda i: (0, 0)),
        ],
        out_specs=[out_spec, out_spec],
        out_shape=[shape, shape],
        compiler_params=params(),
        cost_estimate=cost(2 * count * table.size * lanes, 2 * data.size + 4 * count * rows * lanes),
        name="back_y",
    )(data, table)


def field_kernel(own_ref, recv_ref, table_ref, *out_refs):
    data = jnp.concatenate([own_ref[...], recv_ref[...]], axis=1)
    result = jnp.dot(data, table_ref[...], preferred_element_type=jnp.float32)
    out_refs[-1][...] = result.astype(jnp.bfloat16)


def field_kernel_into(own_ref, recv_ref, table_ref, so_far_ref, out_ref):
    field_kernel(own_ref, recv_ref, table_ref, out_ref)


def field_call(own, recv, table, total, start, rows, so_far):
    step = CHANNEL_STEP
    lanes = own.shape[1]
    columns, cells = table.shape
    count = own.shape[0] // rows
    in_spec = pl.BlockSpec((step * rows, lanes), lambda i: (i, 0))
    operands = [own, recv, table]
    in_specs = [in_spec, in_spec, pl.BlockSpec((columns, cells), lambda i: (0, 0))]
    aliases = {}
    body = field_kernel
    if so_far is not None:
        operands.append(so_far)
        in_specs.append(pl.BlockSpec(memory_space=pl.ANY))
        aliases = {3: 0}
        body = field_kernel_into
    return pl.pallas_call(
        body,
        grid=(count // step,),
        in_specs=in_specs,
        out_specs=pl.BlockSpec((step * rows, cells), lambda i: (start // step + i, 0)),
        out_shape=jax.ShapeDtypeStruct((total * rows, cells), jnp.bfloat16),
        input_output_aliases=aliases,
        compiler_params=params(),
        cost_estimate=cost(2 * count * rows * columns * cells, 2 * count * rows * (columns + cells)),
        name="field",
    )(*operands)


def fast_shards(layer_input, output_cotangent, spectral_weight):
    channels, local_x, local_y, cells = layer_input.shape[1:]
    wide = lax.axis_size("wide")
    rows = local_x * local_y
    me = lax.axis_index("narrow")
    swap = [(0, 1), (1, 0)]
    orders = ((0, 1), (1, 0))
    plain, doubled, inverse = zip(*(zt_tables(list(order)) for order in orders))
    forward_y, back_y = zip(*(y_tables(order, local_y, local_x) for order in orders))
    plain, doubled, inverse = pick(plain, me), pick(doubled, me), pick(inverse, me)
    forward_y, back_y = pick(forward_y, me), pick(back_y, me)
    forward_x, back_x = (jnp.asarray(table) for table in x_tables())
    pairs = plain.shape[1] // 4

    def flat(field):
        return jnp.transpose(field[0], (0, 2, 1, 3)).reshape(channels * rows, cells)

    def to_modes(field, table, chunks):
        count = channels // chunks
        outs = []
        for start in range(0, channels, count):
            own, other = plane_call(field, table, start, count, rows)
            recv = lax.ppermute(other, "narrow", swap)
            line = line_call(own, recv, forward_y, wide, rows)
            line = lax.all_to_all(line, "wide", split_axis=0, concat_axis=0, tiled=True)
            outs.append(spec_call(line, forward_x, local_x))
        return outs[0] if chunks == 1 else jnp.concatenate(outs, axis=2)

    grad_spec = to_modes(flat(output_cotangent), doubled, GRAD_CHUNKS)
    input_spec = to_modes(flat(layer_input), plain, INPUT_CHUNKS)
    kept = grad_spec.shape[0]
    weight = jnp.transpose(spectral_weight[0], (1, 2, 3, 4, 0))
    dual = dual_call(weight, grad_spec)

    def both(spec):
        n_rep = lax.axis_size("rep")
        halves = spec.reshape((n_rep, kept // n_rep) + spec.shape[1:])
        return lax.all_to_all(halves, "rep", split_axis=0, concat_axis=0, tiled=True)

    weight_grad = outer_call(both(input_spec), both(grad_spec))
    weight_grad = jnp.transpose(weight_grad, (4, 0, 1, 2, 3))

    count = channels // BACK_CHUNKS
    result = None
    for start in range(0, channels, count):
        block = back_x_call(dual, back_x, wide, local_x, pairs, start, count)
        block = lax.all_to_all(block, "wide", split_axis=0, concat_axis=0, tiled=True)
        own, other = back_y_call(block, back_y, rows)
        recv = lax.ppermute(other, "narrow", swap)
        result = field_call(own, recv, inverse, channels, start, rows, result)
    field = result.reshape(channels, local_y, local_x, cells)
    return (jnp.transpose(field, (0, 2, 1, 3))[None], weight_grad[None])


def aligned(mesh):
    wide, narrow = mesh.shape["wide"], mesh.shape["narrow"]
    return narrow == 2 and (2 * MY) % wide == 0 and (NX // wide) % 16 == 0 and NY % narrow == 0


def solution(mesh):
    in_specs = (
        P("rep", None, "wide", "narrow", None),
        P("rep", None, "wide", "narrow", None),
        P("narrow", "wide", None, None, None, None),
    )
    out_specs = (
        P("rep", None, "wide", "narrow", None),
        P("narrow", "wide", "rep", None, None, None),
    )
    body = fast_shards if aligned(mesh) else shards
    return jax.shard_map(body, mesh=mesh, in_specs=in_specs, out_specs=out_specs, check_vma=False)
```

```python
import functools
import math

import jax
import jax.numpy as jnp
import ml_dtypes
import numpy as np
from jax import lax
from jax.experimental import pallas as pl
from jax.experimental.pallas import tpu as pltpu
from jax.sharding import PartitionSpec as P

MX = 12
MY = 12
MZ = 16
MT = 4
NX = 128
NY = 44
NZ = 64
NT = 16

CHANNEL_STEP = 4
CHUNKS = 2
VMEM_BYTES = 48 * 1024 * 1024


def kept_waves(length, modes):
    indices = jnp.arange(2 * modes, dtype=jnp.int32)
    return jnp.where(indices < modes, indices, indices + length - 2 * modes)


def phase_pair(length, modes):
    positions = jnp.arange(length, dtype=jnp.int32)
    phase_turns = positions[:, None] * kept_waves(length, modes)[None, :] % length
    phases = 2.0 * math.pi / length * phase_turns.astype(jnp.float32)
    return (jnp.cos(phases), jnp.sin(phases))


def forward_table(length, modes):
    cosine, sine_part = phase_pair(length, modes)
    twiddle = jnp.stack(
        [jnp.stack([cosine, -sine_part], axis=-1), jnp.stack([sine_part, cosine], axis=-1)], axis=1
    )
    return twiddle.astype(jnp.bfloat16)


def inverse_table(length, modes):
    cosine, sine_part = phase_pair(length, modes)
    cos_rows = cosine.T
    sin_rows = sine_part.T
    twiddle = jnp.stack(
        [jnp.stack([cos_rows, sin_rows], axis=-1), jnp.stack([-sin_rows, cos_rows], axis=-1)],
        axis=1,
    )
    return twiddle.astype(jnp.bfloat16)


def plane_tables():
    positions = jnp.arange(NZ * NT, dtype=jnp.int32)
    depth_index = positions // NT
    moment = positions % NT
    pair_index = jnp.arange(2 * MZ * MT, dtype=jnp.int32)
    wave_z = kept_waves(NZ, MZ)[pair_index // MT]
    wave_t = pair_index % MT
    phase_turns = (
        depth_index[:, None] * wave_z[None, :] % NZ * NT
        + moment[:, None] * wave_t[None, :] % NT * NZ
    ) % (NZ * NT)
    phases = 2.0 * math.pi / (NZ * NT) * phase_turns.astype(jnp.float32)
    norm_scale = 1.0 / math.sqrt(NX * NY * NZ * NT)
    cosine = norm_scale * jnp.cos(phases)
    sine_part = norm_scale * jnp.sin(phases)
    forward = jnp.concatenate([cosine, -sine_part], axis=1).astype(jnp.bfloat16)
    inverse = jnp.concatenate([cosine.T, -sine_part.T], axis=0).astype(jnp.bfloat16)
    doubled = jnp.where(wave_t == 0, 1.0, 2.0).astype(jnp.float32)
    factor = jnp.concatenate([doubled, doubled])
    return (forward, inverse, factor)


def outer_terms(input_spec, grad_spec):
    in_real = input_spec[..., 0, :].astype(jnp.float32)[..., :, None]
    in_imag = input_spec[..., 1, :].astype(jnp.float32)[..., :, None]
    grad_real = grad_spec[..., 0, :].astype(jnp.float32)[..., None, :]
    grad_imag = grad_spec[..., 1, :].astype(jnp.float32)[..., None, :]
    real_part = in_real * grad_real + in_imag * grad_imag
    imag_part = in_real * grad_imag - in_imag * grad_real
    return jnp.stack([real_part, imag_part], axis=-3)


def shards(layer_input, output_cotangent, spectral_weight):
    input_field = layer_input[0]
    grad_field = output_cotangent[0]
    channels, local_x, local_y, plane_cells = grad_field.shape
    pair_count = 2 * MZ * MT
    forward, inverse, factor = plane_tables()
    input_plane = jnp.dot(
        input_field.reshape(-1, plane_cells), forward, preferred_element_type=jnp.float32
    )
    input_plane = input_plane.astype(jnp.bfloat16).reshape(
        channels, local_x, local_y, 2, pair_count
    )
    grad_plane = (
        jnp.dot(grad_field.reshape(-1, plane_cells), forward, preferred_element_type=jnp.float32)
        * factor
    )
    grad_plane = grad_plane.astype(jnp.bfloat16).reshape(channels, local_x, local_y, 2, pair_count)
    table_y = forward_table(NY, MY)
    fields = (
        lax.all_to_all(input_plane, "narrow", split_axis=4, concat_axis=2, tiled=True),
        lax.all_to_all(grad_plane, "narrow", split_axis=4, concat_axis=2, tiled=True),
    )
    input_line, grad_line = tuple(
        (
            jnp.einsum(
                "cxyrm,yrjs->cxsjm", field, table_y, preferred_element_type=jnp.float32
            ).astype(jnp.bfloat16)
            for field in fields
        )
    )
    combos = input_line.shape[3] * input_line.shape[4]
    input_flat = input_line.reshape(channels, local_x, 2, combos)
    grad_flat = grad_line.reshape(channels, local_x, 2, combos)
    table_x = forward_table(NX, MX)
    back_table_x = inverse_table(NX, MX)
    back_table_y = inverse_table(NY, MY)
    fields = (
        lax.all_to_all(input_flat, "wide", split_axis=3, concat_axis=1, tiled=True),
        lax.all_to_all(grad_flat, "wide", split_axis=3, concat_axis=1, tiled=True),
    )
    input_spec, grad_spec = tuple(
        (
            jnp.einsum(
                "cxrq,xrks->qksc", field, table_x, preferred_element_type=jnp.float32
            ).astype(jnp.bfloat16)
            for field in fields
        )
    )
    weight_block = spectral_weight[0]
    weight_real = weight_block[:, :, 0]
    weight_imag = weight_block[:, :, 1]
    grad_real = grad_spec[:, :, 0]
    grad_imag = grad_spec[:, :, 1]

    def contract(left, right):
        return jnp.einsum("qkio,qko->qki", left, right, preferred_element_type=jnp.float32)

    dual_real = contract(weight_real, grad_real) + contract(weight_imag, grad_imag)
    dual_imag = contract(weight_real, grad_imag) - contract(weight_imag, grad_real)
    dual = jnp.stack([dual_real, dual_imag], axis=2).astype(jnp.bfloat16)
    both_input, both_grad = (
        lax.all_gather(input_spec[None], "rep", axis=0, tiled=True),
        lax.all_gather(grad_spec[None], "rep", axis=0, tiled=True),
    )
    half_modes = input_spec.shape[1] // lax.axis_size("rep")
    mode_start = lax.axis_index("rep") * half_modes
    input_half = lax.dynamic_slice_in_dim(both_input, mode_start, half_modes, 2)
    grad_half = lax.dynamic_slice_in_dim(both_grad, mode_start, half_modes, 2)
    weight_grad = jnp.sum(outer_terms(input_half, grad_half), axis=0)
    back_x = jnp.einsum(
        "qksc,ksxr->cxrq", dual, back_table_x, preferred_element_type=jnp.float32
    ).astype(jnp.bfloat16)
    block_part = lax.all_to_all(back_x, "wide", split_axis=1, concat_axis=3, tiled=True)
    shaped = block_part.reshape(block_part.shape[0], local_x, 2, 2 * MY, -1)
    back_line = jnp.einsum(
        "cxsjm,jsyr->cxyrm", shaped, back_table_y, preferred_element_type=jnp.float32
    ).astype(jnp.bfloat16)
    block_part = lax.all_to_all(back_line, "narrow", split_axis=2, concat_axis=4, tiled=True)
    result = jnp.dot(
        block_part.reshape(-1, 2 * pair_count), inverse, preferred_element_type=jnp.float32
    )
    input_grad = result.astype(jnp.bfloat16).reshape(
        block_part.shape[0], local_x, local_y, plane_cells
    )
    return (input_grad[None], weight_grad[None])


def np_phases(length, modes):
    waves = np.arange(2 * modes)
    waves = np.where(waves < modes, waves, waves + length - 2 * modes)
    turns = np.arange(length)[:, None] * waves[None, :] % length
    phases = np.float32(2.0 * math.pi / length) * turns.astype(np.float32)
    return (np.cos(phases), np.sin(phases))


def np_plane(blocks):
    positions = np.arange(NZ * NT)
    pairs = np.arange(2 * MZ * MT)
    waves = np.arange(2 * MZ)
    waves = np.where(waves < MZ, waves, waves + NZ - 2 * MZ)[pairs // MT]
    moments = pairs % MT
    turns = (
        (positions // NT)[:, None] * waves[None, :] % NZ * NT
        + (positions % NT)[:, None] * moments[None, :] % NT * NZ
    ) % (NZ * NT)
    phases = np.float32(2.0 * math.pi / (NZ * NT)) * turns.astype(np.float32)
    scale = np.float32(1.0 / math.sqrt(NX * NY * NZ * NT))
    cells = NZ * NT
    cosine = (scale * np.cos(phases)).reshape(cells, blocks, -1)
    sine = (scale * np.sin(phases)).reshape(cells, blocks, -1)
    factor = np.where(moments == 0, 1.0, 2.0).astype(np.float32).reshape(blocks, -1)
    return cosine, sine, factor


def pick(options, index):
    return lax.dynamic_index_in_dim(jnp.asarray(np.stack(options)), index, 0, keepdims=False)


def bf16(array):
    return np.asarray(array, np.float32).astype(ml_dtypes.bfloat16)


def zt_tables(order):
    cosine, sine, factor = np_plane(len(order))
    both = np.stack([cosine, -sine], axis=2)[:, order]
    plain = bf16(both)
    grad = bf16(plain.astype(np.float32) * factor[order][None, :, None, :])
    cells = both.shape[0]
    plain = plain.reshape(cells, -1)
    return plain, grad.reshape(cells, -1), np.ascontiguousarray(plain.T)


def y_tables(order, local_y, local_x):
    cosine, sine = np_phases(NY, MY)
    both = bf16(np.stack([cosine, sine])).astype(np.float32)
    rows = np.concatenate([np.arange(o * local_y, (o + 1) * local_y) for o in order])
    both = both[:, rows]
    eye = np.eye(local_x, dtype=np.float32)
    forward = np.einsum("ayj,xz->ajxyz", both, eye).reshape(2 * 2 * MY * local_x, -1)
    back = np.einsum("ayj,xz->ayxjz", both, eye).reshape(2 * NY * local_x, -1)
    return bf16(forward), bf16(back)


def x_tables():
    cosine, sine = np_phases(NX, MX)
    forward = np.concatenate([cosine.T, sine.T], axis=0)
    back = np.concatenate([cosine, sine], axis=0)
    return bf16(forward), bf16(back)


def params():
    return pltpu.CompilerParams(vmem_limit_bytes=VMEM_BYTES)


def cost(flops, moved):
    return pl.CostEstimate(flops=int(flops), bytes_accessed=int(moved), transcendentals=0)


def call(body, operands, in_specs, after, **settings):
    held_back = len(operands)
    if after is None:
        return pl.pallas_call(body, in_specs=in_specs, **settings)(*operands)

    def without(*refs):
        body(*refs[:held_back], *refs[held_back + 1 :])

    specs = list(in_specs) + [pl.BlockSpec(memory_space=pl.ANY)]
    return pl.pallas_call(without, in_specs=specs, **settings)(*operands, after)


def signs(shape, first):
    lane = lax.broadcasted_iota(jnp.int32, shape, 1)
    return jnp.where(lane < shape[1] // 2, first, -first).astype(jnp.float32)


def half_turn(array):
    return pltpu.roll(array, array.shape[1] // 2, 1)


def plane_kernel(field_ref, table_ref, own_ref, other_ref):
    lanes = own_ref.shape[1]
    result = jnp.dot(field_ref[...], table_ref[...], preferred_element_type=jnp.float32)
    result = result.astype(jnp.bfloat16)
    own_ref[...] = result[:, :lanes]
    other_ref[...] = result[:, lanes:]


def plane_call(field, table, start, count, rows, after=None):
    step = CHANNEL_STEP
    cells, columns = table.shape
    lanes = columns // 2
    shape = jax.ShapeDtypeStruct((count * rows, lanes), jnp.bfloat16)
    out_spec = pl.BlockSpec((step * rows, lanes), lambda i: (i, 0))
    return call(
        plane_kernel,
        [field, table],
        [
            pl.BlockSpec((step * rows, cells), lambda i: (start // step + i, 0)),
            pl.BlockSpec((cells, columns), lambda i: (0, 0)),
        ],
        after,
        grid=(count // step,),
        out_specs=[out_spec, out_spec],
        out_shape=[shape, shape],
        compiler_params=params(),
        cost_estimate=cost(2 * count * rows * cells * columns, 2 * count * rows * (cells + columns)),
        name="plane",
    )


def line_kernel(rows, own_ref, recv_ref, table_ref, out_ref):
    wide, channels, part, lanes = out_ref.shape
    half = wide * part
    sign = signs((half, lanes), 1.0)
    for pair in range(0, channels, 2):
        data = jnp.concatenate(
            [
                jnp.concatenate(
                    [own_ref[c * rows : (c + 1) * rows], recv_ref[c * rows : (c + 1) * rows]], axis=0
                )
                for c in (pair, pair + 1)
            ],
            axis=1,
        )
        result = jnp.dot(table_ref[...], data, preferred_element_type=jnp.float32)
        for at in range(2):
            block = result[:, at * lanes : (at + 1) * lanes]
            line = (block[:half] + sign * half_turn(block[half:])).astype(jnp.bfloat16)
            for w in range(wide):
                out_ref[w, pair + at] = line[w * part : (w + 1) * part]


def line_call(own, recv, table, wide, rows, after=None):
    step = CHANNEL_STEP
    count = own.shape[0] // rows
    lanes = own.shape[1]
    half = table.shape[0] // 2
    in_spec = pl.BlockSpec((step * rows, lanes), lambda i: (i, 0))
    return call(
        functools.partial(line_kernel, rows),
        [own, recv, table],
        [in_spec, in_spec, pl.BlockSpec(table.shape, lambda i: (0, 0))],
        after,
        grid=(count // step,),
        out_specs=pl.BlockSpec((wide, step, half // wide, lanes), lambda i: (0, i, 0, 0)),
        out_shape=jax.ShapeDtypeStruct((wide, count, half // wide, lanes), jnp.bfloat16),
        compiler_params=params(),
        cost_estimate=cost(4 * count * half * table.shape[1] * lanes, 2 * count * lanes * (half + table.shape[1])),
        name="line",
    )


def spec_kernel(local_x, *refs):
    *data_refs, table_ref, out_ref, held = refs
    wide, channels, part, lanes = data_refs[0].shape
    combos = part // local_x
    kept = table_ref.shape[0] // 2
    pairs = lanes // 2
    sign = signs((kept, lanes), 1.0)
    low = lax.broadcasted_iota(jnp.int32, (kept, lanes), 1) < pairs
    for c in range(len(data_refs) * channels):
        data_ref = data_refs[c // channels]
        data = jnp.concatenate(
            [
                jnp.concatenate(
                    [data_ref[w, c % channels, j * local_x : (j + 1) * local_x] for w in range(wide)], axis=0
                )
                for j in range(combos)
            ],
            axis=1,
        )
        result = jnp.dot(table_ref[...], data, preferred_element_type=jnp.float32)
        parts = []
        for j in range(combos):
            block = result[:, j * lanes : (j + 1) * lanes]
            parts.append(block[:kept] + sign * half_turn(block[kept:]))
        for j in range(0, combos - 1, 2):
            first, second = parts[j], parts[j + 1]
            held[:, 0, c, j * pairs : (j + 2) * pairs] = jnp.where(low, first, half_turn(second))
            held[:, 1, c, j * pairs : (j + 2) * pairs] = jnp.where(low, half_turn(first), second)
        if combos % 2:
            j = combos - 1
            held[:, 0, c, j * pairs : (j + 1) * pairs] = parts[j][:, :pairs]
            held[:, 1, c, j * pairs : (j + 1) * pairs] = half_turn(parts[j])[:, :pairs]
    out_ref[...] = held[...].astype(jnp.bfloat16)


def spec_call(chunks, table, local_x, after=None):
    wide, step, part, lanes = chunks[0].shape
    count = len(chunks) * step
    kept = table.shape[0] // 2
    width = part // local_x * lanes // 2
    whole = pl.BlockSpec((wide, step, part, lanes), lambda i: (0, 0, 0, 0))
    return call(
        functools.partial(spec_kernel, local_x),
        [*chunks, table],
        [whole] * len(chunks) + [pl.BlockSpec(table.shape, lambda i: (0, 0))],
        after,
        grid=(1,),
        out_specs=pl.BlockSpec((kept, 2, count, width), lambda i: (0, 0, 0, 0)),
        out_shape=jax.ShapeDtypeStruct((kept, 2, count, width), jnp.bfloat16),
        scratch_shapes=[pltpu.VMEM((kept, 2, count, width), jnp.float32)],
        compiler_params=params(),
        cost_estimate=cost(
            4 * count * kept * table.shape[1] * 2 * width, 2 * wide * count * part * lanes
        ),
        name="spec",
    )


def dual_kernel(last, weight_ref, grad_ref, *refs):
    out_ref = refs[-1]
    inputs = weight_ref.shape[2]
    grad_real = grad_ref[0, 0].astype(jnp.float32)
    grad_imag = grad_ref[0, 1].astype(jnp.float32)
    for i in range(0, inputs, 8):
        real = weight_ref[0, 0, i : i + 8].astype(jnp.float32)
        imag = weight_ref[0, 1, i : i + 8].astype(jnp.float32)
        dual_real = jnp.sum(real * grad_real[None] + imag * grad_imag[None], axis=1)
        dual_imag = jnp.sum(real * grad_imag[None] - imag * grad_real[None], axis=1)
        for s, part in enumerate((dual_real, dual_imag)):
            if len(refs) > 1:
                part = part + refs[0][0, s, i : i + 8]
            if last:
                part = part.astype(jnp.bfloat16).astype(jnp.float32)
            out_ref[0, s, i : i + 8] = part


def dual_call(weight, grad, start, so_far, last, after=None):
    kept, parts, inputs, _, width = weight.shape
    count = grad.shape[2]
    out_spec = pl.BlockSpec((1, parts, inputs, width), lambda k: (k, 0, 0, 0))
    operands = [weight, grad]
    in_specs = [
        pl.BlockSpec((1, parts, inputs, count, width), lambda k: (k, 0, 0, start // count, 0)),
        pl.BlockSpec((1, parts, count, width), lambda k: (k, 0, 0, 0)),
    ]
    if so_far is not None:
        operands.append(so_far)
        in_specs.append(out_spec)
    return call(
        functools.partial(dual_kernel, last),
        operands,
        in_specs,
        after,
        grid=(kept,),
        out_specs=out_spec,
        out_shape=jax.ShapeDtypeStruct((kept, parts, inputs, width), jnp.float32),
        compiler_params=params(),
        cost_estimate=cost(4 * kept * inputs * count * width, 4 * kept * inputs * count * width),
        name="dual",
    )


def outer_kernel(input_ref, grad_ref, out_ref):
    samples = input_ref.shape[0]
    inputs = out_ref.shape[2]
    for i in range(0, inputs, 8):
        real_part = 0.0
        imag_part = 0.0
        for n in range(samples):
            in_real = input_ref[n, 0, 0, i : i + 8].astype(jnp.float32)[:, None, :]
            in_imag = input_ref[n, 0, 1, i : i + 8].astype(jnp.float32)[:, None, :]
            grad_real = grad_ref[n, 0, 0].astype(jnp.float32)[None]
            grad_imag = grad_ref[n, 0, 1].astype(jnp.float32)[None]
            real_part = real_part + (in_real * grad_real + in_imag * grad_imag)
            imag_part = imag_part + (in_real * grad_imag - in_imag * grad_real)
        out_ref[0, 0, i : i + 8] = real_part
        out_ref[0, 1, i : i + 8] = imag_part


def outer_call(both_input, both_grad, after=None):
    samples, kept, parts, channels, width = both_input.shape
    in_spec = pl.BlockSpec((samples, 1, parts, channels, width), lambda k: (0, k, 0, 0, 0))
    out = (kept, parts, channels, channels, width)
    return call(
        outer_kernel,
        [both_input, both_grad],
        [in_spec, in_spec],
        after,
        grid=(kept,),
        out_specs=pl.BlockSpec((1,) + out[1:], lambda k: (k, 0, 0, 0, 0)),
        out_shape=jax.ShapeDtypeStruct(out, jnp.float32),
        compiler_params=params(),
        cost_estimate=cost(8 * math.prod(out), 6 * math.prod(out)),
        name="outer",
    )


def back_x_kernel(local_x, dual_ref, table_ref, out_ref):
    wide, channels, part, lanes = out_ref.shape
    combos = part // local_x
    kept = dual_ref.shape[0]
    pairs = lanes // 2
    cells = wide * local_x
    sign = signs((cells, lanes), -1.0)
    low = lax.broadcasted_iota(jnp.int32, (kept, lanes), 1) < pairs
    for c in range(channels):
        blocks = []
        for j in range(0, combos - 1, 2):
            real = dual_ref[:, 0, c, j * pairs : (j + 2) * pairs]
            imag = dual_ref[:, 1, c, j * pairs : (j + 2) * pairs]
            blocks.append(jnp.where(low, real, half_turn(imag)))
            blocks.append(jnp.where(low, half_turn(real), imag))
        if combos % 2:
            j = combos - 1
            real = dual_ref[:, 0, c, j * pairs : (j + 1) * pairs]
            imag = dual_ref[:, 1, c, j * pairs : (j + 1) * pairs]
            blocks.append(jnp.concatenate([real, imag], axis=1))
        data = jnp.concatenate(blocks, axis=1).astype(jnp.bfloat16)
        result = jnp.dot(table_ref[...], data, preferred_element_type=jnp.float32)
        for j in range(combos):
            block = result[:, j * lanes : (j + 1) * lanes]
            back = (block[:cells] + sign * half_turn(block[cells:])).astype(jnp.bfloat16)
            for w in range(wide):
                out_ref[w, c, j * local_x : (j + 1) * local_x] = back[w * local_x : (w + 1) * local_x]


def back_x_call(dual, table, wide, local_x, pairs, start, count, after=None):
    kept, parts, channels, width = dual.shape
    step = 8
    part = width // pairs * local_x
    lanes = 2 * pairs
    return call(
        functools.partial(back_x_kernel, local_x),
        [dual, table],
        [
            pl.BlockSpec((kept, parts, step, width), lambda i: (0, 0, start // step + i, 0)),
            pl.BlockSpec(table.shape, lambda i: (0, 0)),
        ],
        after,
        grid=(count // step,),
        out_specs=pl.BlockSpec((wide, step, part, lanes), lambda i: (0, i, 0, 0)),
        out_shape=jax.ShapeDtypeStruct((wide, count, part, lanes), jnp.bfloat16),
        compiler_params=params(),
        cost_estimate=cost(4 * count * kept * table.shape[0] * width, 4 * kept * count * width * 2),
        name="back_x",
    )


def back_y_kernel(rows, data_ref, table_ref, own_ref, other_ref):
    wide, channels, part, lanes = data_ref.shape
    half = table_ref.shape[0] // 2
    sign = signs((half, lanes), -1.0)
    for pair in range(0, channels, 2):
        data = jnp.concatenate(
            [
                jnp.concatenate([data_ref[w, c] for w in range(wide)], axis=0)
                for c in (pair, pair + 1)
            ],
            axis=1,
        )
        result = jnp.dot(table_ref[...], data, preferred_element_type=jnp.float32)
        for at in range(2):
            c = pair + at
            block = result[:, at * lanes : (at + 1) * lanes]
            back = (block[:half] + sign * half_turn(block[half:])).astype(jnp.bfloat16)
            own_ref[c * rows : (c + 1) * rows] = back[:rows]
            other_ref[c * rows : (c + 1) * rows] = back[rows:]


def back_y_call(data, table, rows, after=None):
    wide, count, part, lanes = data.shape
    step = CHANNEL_STEP
    shape = jax.ShapeDtypeStruct((count * rows, lanes), jnp.bfloat16)
    out_spec = pl.BlockSpec((step * rows, lanes), lambda i: (i, 0))
    return call(
        functools.partial(back_y_kernel, rows),
        [data, table],
        [
            pl.BlockSpec((wide, step, part, lanes), lambda i: (0, i, 0, 0)),
            pl.BlockSpec(table.shape, lambda i: (0, 0)),
        ],
        after,
        grid=(count // step,),
        out_specs=[out_spec, out_spec],
        out_shape=[shape, shape],
        compiler_params=params(),
        cost_estimate=cost(2 * count * table.size * lanes, 2 * data.size + 4 * count * rows * lanes),
        name="back_y",
    )


def field_kernel(own_ref, recv_ref, table_ref, *out_refs):
    data = jnp.concatenate([own_ref[...], recv_ref[...]], axis=1)
    result = jnp.dot(data, table_ref[...], preferred_element_type=jnp.float32)
    out_refs[-1][...] = result.astype(jnp.bfloat16)


def field_kernel_into(own_ref, recv_ref, table_ref, so_far_ref, out_ref):
    field_kernel(own_ref, recv_ref, table_ref, out_ref)


def field_call(own, recv, table, total, start, rows, so_far, after=None):
    step = CHANNEL_STEP
    lanes = own.shape[1]
    columns, cells = table.shape
    count = own.shape[0] // rows
    in_spec = pl.BlockSpec((step * rows, lanes), lambda i: (i, 0))
    operands = [own, recv, table]
    in_specs = [in_spec, in_spec, pl.BlockSpec((columns, cells), lambda i: (0, 0))]
    aliases = {}
    body = field_kernel
    if so_far is not None:
        operands.append(so_far)
        in_specs.append(pl.BlockSpec(memory_space=pl.ANY))
        aliases = {3: 0}
        body = field_kernel_into
    return call(
        body,
        [*operands],
        in_specs,
        after,
        grid=(count // step,),
        out_specs=pl.BlockSpec((step * rows, cells), lambda i: (start // step + i, 0)),
        out_shape=jax.ShapeDtypeStruct((total * rows, cells), jnp.bfloat16),
        input_output_aliases=aliases,
        compiler_params=params(),
        cost_estimate=cost(2 * count * rows * columns * cells, 2 * count * rows * (columns + cells)),
        name="field",
    )


def fast_shards(layer_input, output_cotangent, spectral_weight):
    channels, local_x, local_y, cells = layer_input.shape[1:]
    wide = lax.axis_size("wide")
    rows = local_x * local_y
    me = lax.axis_index("narrow")
    swap = [(0, 1), (1, 0)]
    orders = ((0, 1), (1, 0))
    plain, doubled, inverse = zip(*(zt_tables(list(order)) for order in orders))
    forward_y, back_y = zip(*(y_tables(order, local_y, local_x) for order in orders))
    plain, doubled, inverse = pick(plain, me), pick(doubled, me), pick(inverse, me)
    forward_y, back_y = pick(forward_y, me), pick(back_y, me)
    forward_x, back_x = (jnp.asarray(table) for table in x_tables())
    pairs = plain.shape[1] // 4

    def flat(field):
        return jnp.transpose(field[0], (0, 2, 1, 3)).reshape(channels * rows, cells)

    count = channels // CHUNKS
    starts = range(0, channels, count)
    kept = forward_x.shape[0] // 2
    weight = jnp.transpose(spectral_weight[0], (1, 2, 3, 4, 0))
    last = None

    def plane(field, table, start):
        nonlocal last
        own, other = plane_call(field, table, start, count, rows, after=last)
        last = own
        return own, lax.ppermute(other, "narrow", swap)

    def line(own, recv):
        nonlocal last
        last = line_call(own, recv, forward_y, wide, rows, after=last)
        return lax.all_to_all(last, "wide", split_axis=0, concat_axis=0, tiled=True)

    def spectrum(chunks):
        nonlocal last
        last = spec_call(chunks, forward_x, local_x, after=last)
        return last

    def back_line(start):
        nonlocal last
        last = back_x_call(dual, back_x, wide, local_x, pairs, start, count, after=last)
        return lax.all_to_all(last, "wide", split_axis=0, concat_axis=0, tiled=True)

    def back_plane(block):
        nonlocal last
        own, other = back_y_call(block, back_y, rows, after=last)
        last = own
        return own, lax.ppermute(other, "narrow", swap)

    def both(spec):
        n_rep = lax.axis_size("rep")
        halves = spec.reshape((n_rep, kept // n_rep) + spec.shape[1:])
        return lax.all_to_all(halves, "rep", split_axis=0, concat_axis=0, tiled=True)

    grad_field, input_field = flat(output_cotangent), flat(layer_input)
    half = CHUNKS // 2
    grad_planes = [plane(grad_field, doubled, start) for start in starts]
    grad_lines = [line(*both_halves) for both_halves in grad_planes[:-1]]
    input_planes = [plane(input_field, plain, starts[0])]
    grad_lines.append(line(*grad_planes[-1]))
    input_planes += [plane(input_field, plain, start) for start in starts[1:half]]
    first_spec = spectrum(grad_lines[:half])
    dual = dual_call(weight, first_spec, 0, None, False, after=last)
    last = dual
    input_planes += [plane(input_field, plain, start) for start in starts[half:]]
    input_lines = [line(*both_halves) for both_halves in input_planes[:half]]
    second_spec = spectrum(grad_lines[half:])
    dual = dual_call(weight, second_spec, channels // 2, dual, True, after=last)
    last = dual
    both_grad = [both(spec) for spec in (first_spec, second_spec)]
    blocks = [back_line(start) for start in starts]
    back_planes = []
    for at, block in enumerate(blocks):
        back_planes.append(back_plane(block))
        if half <= at + half // 2 + 1 and len(input_lines) < CHUNKS:
            input_lines.append(line(*input_planes[len(input_lines)]))
    result = None
    for start, both_halves in zip(starts, back_planes):
        result = field_call(*both_halves, inverse, channels, start, rows, result, after=last)
        last = both_halves[0]
    input_specs = [both(spectrum(input_lines[:half])), both(spectrum(input_lines[half:]))]
    both_input = jnp.concatenate(input_specs, axis=3)
    weight_grad = outer_call(both_input, jnp.concatenate(both_grad, axis=3))
    weight_grad = jnp.transpose(weight_grad, (4, 0, 1, 2, 3))
    field = result.reshape(channels, local_y, local_x, cells)
    return (jnp.transpose(field, (0, 2, 1, 3))[None], weight_grad[None])


def aligned(mesh):
    wide, narrow = mesh.shape["wide"], mesh.shape["narrow"]
    return narrow == 2 and (2 * MY) % wide == 0 and (NX // wide) % 16 == 0 and NY % narrow == 0


def solution(mesh):
    in_specs = (
        P("rep", None, "wide", "narrow", None),
        P("rep", None, "wide", "narrow", None),
        P("narrow", "wide", None, None, None, None),
    )
    out_specs = (
        P("rep", None, "wide", "narrow", None),
        P("narrow", "wide", "rep", None, None, None),
    )
    body = fast_shards if aligned(mesh) else shards
    return jax.shard_map(body, mesh=mesh, in_specs=in_specs, out_specs=out_specs, check_vma=False)
```
